32 devices in a mesh: rep: 8 (over y, x, core), blk: 4 (over z).
Axes of the slice: x: 2, y: 2, z: 4, core: 2. Of those that a mesh axis runs over, the one named last changes fastest.
Arguments:
- green_samples: bfloat16 [128, 2, 128, 128], P(('rep', 'blk')), may hold values from -0.4453125 to 0.4453125
- exchange_index_order: int32 [16, 128], P('blk'), may hold values from 0 to 127, each once within a row
- frequency_offset: int32 [16], P('blk'), may hold values from 0 to 127
Outputs:
- vertex: float32 [2, 16, 128, 128], P(None, 'blk', 'rep')
The draws below stay inside these ranges and needn't reach their ends.
Inputs may be any that keep to these rules, and one draw needn't show every extreme that they name: Each row of exchange_index_order names every index of 0 to 127 once.
All inputs are finite; a program needn't handle non-finite values.
Results may differ from the reference program's by a relative error of at most 0.0003.
Values may be sent and summed in bfloat16 or wider, within the bound.
No kernel may reach another device: no remote copies, remote signals or barrier semaphores. Data moves between devices by JAX's collectives and lax.ppermute only.
A program may use at most 128 MiB of HBM per device.

```python
import jax
import jax.numpy as jnp
from jax import lax

COMBINED_INDEX = 128
Q = 16
MEASURE_COUNT = 128


def with_ends(result, key, low, largest):
    spot = [jax.random.randint(jax.random.fold_in(key, axis), (), 0, length) for axis, length in enumerate(result.shape)]
    main_axis = result.shape.index(max(result.shape))
    next_to = spot[:main_axis] + [(spot[main_axis] + 1) % result.shape[main_axis]] + spot[main_axis + 1:]
    return result.at[tuple(spot)].set(low).at[tuple(next_to)].set(largest)


def block_levels(key, dims, shards, low, largest):
    loudness = 1.0
    for dim, shards_of in shards:
        draws = jax.random.uniform(jax.random.fold_in(jax.random.fold_in(key, 6), dim), (shards_of,), jnp.float32, low / len(shards), largest / len(shards))
        loudness = loudness * jnp.repeat(jnp.exp(draws), dims[dim] // shards_of).reshape((-1,) + (1,) * (len(dims) - 1 - dim))
    return loudness


def normal_values(rng, dims, spread, most, pieces=(), kind=jnp.bfloat16):
    loudness = block_levels(rng, dims, pieces, -0.22, 0.18) if pieces else 1.0
    drawn = jax.random.normal(rng, dims, jnp.float32) * spread * loudness
    return jnp.minimum(jnp.maximum(drawn, -most), most).astype(kind)


def setup_inputs(seed: int = 0) -> dict:
    splits = jax.random.split(jax.random.key(seed), 4)
    return {
        "green_samples": normal_values(splits[0], (MEASURE_COUNT, 2, COMBINED_INDEX, COMBINED_INDEX), (1.0 / (2 * COMBINED_INDEX * MEASURE_COUNT) ** 0.25), 0.4453125, ((0, 32),)),
        "exchange_index_order": jax.vmap(lambda own: jax.random.permutation(own, COMBINED_INDEX))(jax.random.split(splits[1], Q)).reshape((Q, COMBINED_INDEX)).astype(jnp.int32),
        "frequency_offset": with_ends(jax.random.randint(splits[2], (Q,), 0, COMBINED_INDEX), jax.random.fold_in(splits[2], 1), 0, COMBINED_INDEX - 1).astype(jnp.int32),
    }


def reference(green_samples, exchange_index_order, frequency_offset):
    green_propagator = green_samples.astype(jnp.float32)
    positions = jnp.arange(COMBINED_INDEX, dtype=jnp.int32)

    def one_tile(index_pair):
        perm_row, shift_val = index_pair
        left = jnp.take(green_propagator, perm_row, axis=3)
        rows = (positions + shift_val) % COMBINED_INDEX
        right = jnp.take(green_propagator, rows, axis=2)
        real_part = jnp.einsum("mik,mkj->ij", left[:, 0], right[:, 0]) - jnp.einsum("mik,mkj->ij", left[:, 1], right[:, 1])
        imag_part = jnp.einsum("mik,mkj->ij", left[:, 0], right[:, 1]) + jnp.einsum("mik,mkj->ij", left[:, 1], right[:, 0])
        return jnp.stack([real_part, imag_part])

    tiles = lax.map(one_tile, (exchange_index_order, frequency_offset))
    return jnp.transpose(tiles, (1, 0, 2, 3)).astype(jnp.float32)
```

```python
import functools

import jax
import jax.numpy as jnp
from jax import lax
from jax.experimental import pallas as pl
from jax.experimental.pallas import tpu as pltpu
from jax.sharding import PartitionSpec as P

VMEM_BYTES = 48 * 1024 * 1024


def plain_body(green_samples, exchange_index_order, frequency_offset):
    tile_width = green_samples.shape[2]
    positions = jnp.arange(tile_width, dtype=jnp.int32)
    back_rows = (positions[None, :] - frequency_offset[:, None]) % tile_width
    composed_cols = jnp.take_along_axis(exchange_index_order, back_rows, axis=1)
    left_table = (composed_cols[:, None, :] == positions[None, :, None]).astype(jnp.bfloat16)
    tile_portion = lax.all_gather(green_samples, "blk", axis=0, tiled=True)
    left = jnp.einsum(
        "mcis,qsk->mciqk", tile_portion, left_table, preferred_element_type=jnp.float32
    ).astype(jnp.bfloat16)
    dot = functools.partial(jnp.einsum, "miqk,mkj->qij", preferred_element_type=jnp.float32)
    real_part = dot(left[:, 0], tile_portion[:, 0]) - dot(left[:, 1], tile_portion[:, 1])
    imag_part = dot(left[:, 0], tile_portion[:, 1]) + dot(left[:, 1], tile_portion[:, 0])
    stacked = jnp.stack([real_part, imag_part])
    return lax.psum_scatter(stacked, "rep", scatter_dimension=2, tiled=True)


def partial_tiles_kernel(
    rep, rows, tiles, order_refs, shift_refs, sample_refs, sum_in, out_refs, table, picked, left, right, total
):
    width = table.shape[0]
    mine = lax.axis_index("rep")
    owners = rep // 2
    block = owners * rows
    columns = lax.broadcasted_iota(jnp.int32, (width, width), 0)
    for group, (order, shift) in enumerate(zip(order_refs, shift_refs)):
        names = order[...]
        for tile in range(tiles):
            turned = pltpu.roll(names, shift[tiles + tile, 0], 1)[tile : tile + 1, :]
            place = (group * tiles + tile) * width
            hot = jnp.where(columns == turned, 1.0, 0.0).astype(jnp.bfloat16)
            table[:, place : place + width] = hot
    count = sample_refs[0].shape[0]
    tile_count = len(order_refs) * tiles
    for source, samples in enumerate(sample_refs):
        for sample in range(count):
            at = source * count + sample
            for part in range(2):
                for step in range(owners):
                    owner = (((mine // 2) ^ step) * 2 + mine % 2) * rows
                    picked[part * block + step * rows : part * block + (step + 1) * rows, :] = samples[
                        sample, part, pl.ds(pl.multiple_of(owner, rows), rows), :
                    ]
            real, imag = samples[sample, 0], samples[sample, 1]
            deep = at * 2 * width
            right[deep : deep + width, :width] = real
            right[deep : deep + width, width:] = imag
            right[deep + width : deep + 2 * width, :width] = -imag
            right[deep + width : deep + 2 * width, width:] = real
            moved = jnp.dot(picked[...], table[...], preferred_element_type=jnp.float32).astype(jnp.bfloat16)
            for tile in range(tile_count):
                for part in range(2):
                    left[tile * block : (tile + 1) * block, deep + part * width : deep + (part + 1) * width] = moved[
                        part * block : (part + 1) * block, tile * width : (tile + 1) * width
                    ]
    sums = jnp.dot(left[...], right[...], preferred_element_type=jnp.float32)
    if sum_in is not None:
        sums = sums + sum_in[...]
    total[...] = sums
    if out_refs is not None:
        for group in range(len(order_refs)):
            for step in range(owners):
                for tile in range(tiles):
                    start = (group * tiles + tile) * block + step * rows
                    out_refs[group][step][tile * rows : (tile + 1) * rows, :] = total[start : start + rows, :]


def partial_tiles(rep, rows, tiles, packs, sources, sum_in, last):
    groups, owners = len(packs), rep // 2
    width = packs[0].shape[1]
    count = sources[0].shape[0]
    depth = len(sources) * count * 2 * width
    block = owners * rows
    height = groups * tiles * block

    def kernel(*refs):
        refs = list(refs)
        orders = [refs.pop(0) for _ in range(groups)]
        shifts = [refs.pop(0) for _ in range(groups)]
        samples = [refs.pop(0) for _ in sources]
        before = refs.pop(0) if sum_in is not None else None
        outs = None
        if last:
            outs = [[refs.pop(0) for _ in range(owners)] for _ in range(groups)]
            total = refs.pop()
        else:
            total = refs.pop(0)
        partial_tiles_kernel(rep, rows, tiles, orders, shifts, samples, before, outs, *refs, total)

    scratch = [
        pltpu.VMEM((width, groups * tiles * width), jnp.bfloat16),
        pltpu.VMEM((2 * block, width), jnp.bfloat16),
        pltpu.VMEM((height, depth), jnp.bfloat16),
        pltpu.VMEM((depth, 2 * width), jnp.bfloat16),
    ]
    if last:
        out_shape = [jax.ShapeDtypeStruct((tiles * rows, 2 * width), jnp.float32)] * (groups * owners)
        scratch.append(pltpu.VMEM((height, 2 * width), jnp.float32))
    else:
        out_shape = [jax.ShapeDtypeStruct((height, 2 * width), jnp.float32)]
    whole = pl.BlockSpec(memory_space=pltpu.VMEM)
    scalars = pl.BlockSpec(memory_space=pltpu.SMEM)
    sums = [] if sum_in is None else [sum_in]
    in_specs = [whole] * groups + [scalars] * groups + [whole] * (len(sources) + len(sums))
    got = pl.pallas_call(
        kernel,
        out_shape=out_shape,
        in_specs=in_specs,
        out_specs=[whole] * len(out_shape),
        scratch_shapes=scratch,
        compiler_params=pltpu.CompilerParams(vmem_limit_bytes=VMEM_BYTES),
        cost_estimate=pl.CostEstimate(
            flops=2 * height * depth * 2 * width * 2, bytes_accessed=2 * depth * width, transcendentals=0
        ),
    )(*packs, *packs, *sources, *sums)
    if not last:
        return got[0]
    return [got[group * owners : (group + 1) * owners] for group in range(groups)]


def body(rep, blk, green_samples, exchange_index_order, frequency_offset):
    tiles, width = exchange_index_order.shape
    rows = width // rep

    def over(axis, size, flip, value):
        return lax.ppermute(value, axis, [(i, i ^ flip) for i in range(size)])

    pack = jnp.concatenate(
        [exchange_index_order, jnp.broadcast_to(frequency_offset[:, None], (tiles, width))]
    )
    near = over("blk", blk, 1, green_samples)
    far_pack = over("blk", blk, 2, pack)
    twin = over("rep", rep, 1, green_samples)
    near_twin = over("rep", rep, 1, near)
    packs = [far_pack, pack]
    sums = partial_tiles(rep, rows, tiles, packs, [green_samples, twin], None, False)
    far_parts, own_parts = partial_tiles(rep, rows, tiles, packs, [near, near_twin], sums, True)

    def collect(parts):
        value = parts[0]
        for step in range(1, rep // 2):
            value = value + over("rep", rep, 2 * step, parts[step])
        return value

    far = over("blk", blk, 2, collect(far_parts))
    done = collect(own_parts) + far
    done = done.reshape(tiles, rows, 2, width)
    return jnp.transpose(done, (2, 0, 1, 3))


def solution(mesh):
    rep, blk = mesh.shape["rep"], mesh.shape["blk"]
    placed = (P(("rep", "blk"), None, None, None), P("blk", None), P("blk"))

    def program(green_samples, exchange_index_order, frequency_offset):
        width = exchange_index_order.shape[1]
        if blk == 4 and width // rep % 16 == 0:
            part = functools.partial(body, rep, blk)
        else:
            part = plain_body
        return jax.shard_map(
            part, mesh=mesh, in_specs=placed, out_specs=P(None, "blk", "rep", None), check_vma=False
        )(green_samples, exchange_index_order, frequency_offset)

    return program
```

```python
import functools

import jax
import jax.numpy as jnp
from jax import lax
from jax.experimental import pallas as pl
from jax.experimental.pallas import tpu as pltpu
from jax.sharding import PartitionSpec as P

VMEM_BYTES = 48 * 1024 * 1024


def plain_body(green_samples, exchange_index_order, frequency_offset):
    tile_width = green_samples.shape[2]
    positions = jnp.arange(tile_width, dtype=jnp.int32)
    back_rows = (positions[None, :] - frequency_offset[:, None]) % tile_width
    composed_cols = jnp.take_along_axis(exchange_index_order, back_rows, axis=1)
    left_table = (composed_cols[:, None, :] == positions[None, :, None]).astype(jnp.bfloat16)
    tile_portion = lax.all_gather(green_samples, "blk", axis=0, tiled=True)
    left = jnp.einsum(
        "mcis,qsk->mciqk", tile_portion, left_table, preferred_element_type=jnp.float32
    ).astype(jnp.bfloat16)
    dot = functools.partial(jnp.einsum, "miqk,mkj->qij", preferred_element_type=jnp.float32)
    real_part = dot(left[:, 0], tile_portion[:, 0]) - dot(left[:, 1], tile_portion[:, 1])
    imag_part = dot(left[:, 0], tile_portion[:, 1]) + dot(left[:, 1], tile_portion[:, 0])
    stacked = jnp.stack([real_part, imag_part])
    return lax.psum_scatter(stacked, "rep", scatter_dimension=2, tiled=True)


def turned_order(order, offset):
    tiles, _ = order.shape

    def kernel(order_ref, offset_ref, out_ref):
        names = order_ref[...]
        for tile in range(tiles):
            out_ref[tile : tile + 1, :] = pltpu.roll(names, offset_ref[tile], 1)[tile : tile + 1, :]

    return pl.pallas_call(
        kernel,
        out_shape=jax.ShapeDtypeStruct(order.shape, order.dtype),
        in_specs=[pl.BlockSpec(memory_space=pltpu.VMEM), pl.BlockSpec(memory_space=pltpu.SMEM)],
        out_specs=pl.BlockSpec(memory_space=pltpu.VMEM),
    )(order, offset)


def partial_tiles(rep, rows, tiles, groups, sources, split):
    owners = rep // 2
    width = groups[0][0].shape[1]
    count = sources[0].shape[0]
    block = owners * rows
    height = tiles * block
    step_deep = count * 2 * width
    depth = len(sources) * step_deep

    def kernel(*refs):
        refs = list(refs)
        orders = [refs.pop(0) for _ in groups]
        befores = [None if group[1] is None else refs.pop(0) for group in groups]
        samples = [refs.pop(0) for _ in sources]
        outs = [[refs.pop(0) for _ in range(owners if split else 1)] for _ in groups]
        table, picked, left, right, total = refs
        mine = lax.axis_index("rep")
        columns = lax.broadcasted_iota(jnp.int32, (width, width), 0)
        for group, order in enumerate(orders):
            names = order[...]
            for tile in range(tiles):
                place = (group * tiles + tile) * width
                hot = jnp.where(columns == names[tile : tile + 1, :], 1.0, 0.0).astype(jnp.bfloat16)
                table[:, place : place + width] = hot
        for source, sample_ref in enumerate(samples):
            used = [group for group in range(len(groups)) if groups[group][2] <= source]
            for sample in range(count):
                for part in range(2):
                    for step in range(owners):
                        owner = (((mine // 2) ^ step) * 2 + mine % 2) * rows
                        picked[part * block + step * rows : part * block + (step + 1) * rows, :] = sample_ref[
                            sample, part, pl.ds(pl.multiple_of(owner, rows), rows), :
                        ]
                real, imag = sample_ref[sample, 0], sample_ref[sample, 1]
                deep = source * step_deep + sample * 2 * width
                right[deep : deep + width, :width] = real
                right[deep : deep + width, width:] = imag
                right[deep + width : deep + 2 * width, :width] = -imag
                right[deep + width : deep + 2 * width, width:] = real
                for group in used:
                    moved = jnp.dot(
                        picked[...],
                        table[:, group * tiles * width : (group + 1) * tiles * width],
                        preferred_element_type=jnp.float32,
                    ).astype(jnp.bfloat16)
                    for tile in range(tiles):
                        for part in range(2):
                            left[
                                group * height + tile * block : group * height + (tile + 1) * block,
                                deep + part * width : deep + (part + 1) * width,
                            ] = moved[part * block : (part + 1) * block, tile * width : (tile + 1) * width]
        for group, (_, _, first) in enumerate(groups):
            start = first * step_deep
            sums = jnp.dot(
                left[group * height : (group + 1) * height, start:], right[start:, :], preferred_element_type=jnp.float32
            )
            if befores[group] is not None:
                sums = sums + befores[group][...]
            if not split:
                outs[group][0][...] = sums
                continue
            total[...] = sums
            for step in range(owners):
                for tile in range(tiles):
                    at = tile * block + step * rows
                    outs[group][step][tile * rows : (tile + 1) * rows, :] = total[at : at + rows, :]

    if split:
        out_shape = [jax.ShapeDtypeStruct((tiles * rows, 2 * width), jnp.float32)] * (len(groups) * owners)
    else:
        out_shape = [jax.ShapeDtypeStruct((height, 2 * width), jnp.float32)] * len(groups)
    operands = [group[0] for group in groups] + [group[1] for group in groups if group[1] is not None] + sources
    whole = pl.BlockSpec(memory_space=pltpu.VMEM)
    got = pl.pallas_call(
        kernel,
        out_shape=out_shape,
        in_specs=[whole] * len(operands),
        out_specs=[whole] * len(out_shape),
        scratch_shapes=[
            pltpu.VMEM((width, len(groups) * tiles * width), jnp.bfloat16),
            pltpu.VMEM((2 * block, width), jnp.bfloat16),
            pltpu.VMEM((len(groups) * height, depth), jnp.bfloat16),
            pltpu.VMEM((depth, 2 * width), jnp.bfloat16),
            pltpu.VMEM((height, 2 * width), jnp.float32),
        ],
        compiler_params=pltpu.CompilerParams(vmem_limit_bytes=VMEM_BYTES),
        cost_estimate=pl.CostEstimate(
            flops=4 * len(groups) * height * depth * 2 * width, bytes_accessed=2 * depth * width, transcendentals=0
        ),
    )(*operands)
    per = owners if split else 1
    got = [got[group * per : (group + 1) * per] for group in range(len(groups))]
    return got if split else [each[0] for each in got]


def body(rep, blk, green_samples, exchange_index_order, frequency_offset):
    tiles, width = exchange_index_order.shape
    rows = width // rep

    def over(axis, size, flip, value):
        return lax.ppermute(value, axis, [(i, i ^ flip) for i in range(size)])

    part = functools.partial(partial_tiles, rep, rows, tiles)
    near = over("blk", blk, 1, green_samples)
    twin = over("rep", rep, 1, green_samples)
    own_order = turned_order(exchange_index_order, frequency_offset)
    far_order = over("blk", blk, 2, own_order)
    (own,) = part([(own_order, None, 0)], [green_samples, twin], False)
    near, own, far_order = lax.optimization_barrier((near, own, far_order))
    near_twin = over("rep", rep, 1, near)
    far, own = part([(far_order, None, 0), (own_order, own, 2)], [green_samples, twin, near], False)
    (far_parts,) = part([(far_order, far, 0)], [near_twin], True)
    (own_parts,) = part([(own_order, own, 0)], [near_twin], True)

    def collect(parts):
        value = parts[0]
        for step in range(1, rep // 2):
            value = value + over("rep", rep, 2 * step, parts[step])
        return value

    far = over("blk", blk, 2, collect(far_parts))
    done = collect(own_parts) + far
    done = done.reshape(tiles, rows, 2, width)
    return jnp.transpose(done, (2, 0, 1, 3))


def solution(mesh):
    rep, blk = mesh.shape["rep"], mesh.shape["blk"]
    placed = (P(("rep", "blk"), None, None, None), P("blk", None), P("blk"))

    def program(green_samples, exchange_index_order, frequency_offset):
        width = exchange_index_order.shape[1]
        if blk == 4 and width // rep % 16 == 0:
            part = functools.partial(body, rep, blk)
        else:
            part = plain_body
        return jax.shard_map(
            part, mesh=mesh, in_specs=placed, out_specs=P(None, "blk", "rep", None), check_vma=False
        )(green_samples, exchange_index_order, frequency_offset)

    return program
```

```python
import functools

import jax
import jax.numpy as jnp
from jax import lax
from jax.experimental import pallas as pl
from jax.experimental.pallas import tpu as pltpu
from jax.sharding import PartitionSpec as P

VMEM_BYTES = 48 * 1024 * 1024


def plain_body(green_samples, exchange_index_order, frequency_offset):
    tile_width = green_samples.shape[2]
    positions = jnp.arange(tile_width, dtype=jnp.int32)
    back_rows = (positions[None, :] - frequency_offset[:, None]) % tile_width
    composed_cols = jnp.take_along_axis(exchange_index_order, back_rows, axis=1)
    left_table = (composed_cols[:, None, :] == positions[None, :, None]).astype(jnp.bfloat16)
    tile_portion = lax.all_gather(green_samples, "blk", axis=0, tiled=True)
    left = jnp.einsum(
        "mcis,qsk->mciqk", tile_portion, left_table, preferred_element_type=jnp.float32
    ).astype(jnp.bfloat16)
    dot = functools.partial(jnp.einsum, "miqk,mkj->qij", preferred_element_type=jnp.float32)
    real_part = dot(left[:, 0], tile_portion[:, 0]) - dot(left[:, 1], tile_portion[:, 1])
    imag_part = dot(left[:, 0], tile_portion[:, 1]) + dot(left[:, 1], tile_portion[:, 0])
    stacked = jnp.stack([real_part, imag_part])
    return lax.psum_scatter(stacked, "rep", scatter_dimension=2, tiled=True)


def turned_order(order, offset):
    tiles, _ = order.shape

    def kernel(order_ref, offset_ref, out_ref):
        names = order_ref[...]
        for tile in range(tiles):
            out_ref[tile : tile + 1, :] = pltpu.roll(names, offset_ref[tile], 1)[tile : tile + 1, :]

    return pl.pallas_call(
        kernel,
        out_shape=jax.ShapeDtypeStruct(order.shape, order.dtype),
        in_specs=[pl.BlockSpec(memory_space=pltpu.VMEM), pl.BlockSpec(memory_space=pltpu.SMEM)],
        out_specs=pl.BlockSpec(memory_space=pltpu.VMEM),
    )(order, offset)


def partial_tiles(rep, rows, tiles, groups, sources, split):
    owners = rep // 2
    width = groups[0][0].shape[1]
    count = sources[0].shape[0]
    block = owners * rows
    height = tiles * block
    step_deep = count * 2 * width
    depth = len(sources) * step_deep

    def kernel(*refs):
        refs = list(refs)
        orders = [refs.pop(0) for _ in groups]
        befores = [None if group[1] is None else refs.pop(0) for group in groups]
        samples = [refs.pop(0) for _ in sources]
        outs = [[refs.pop(0) for _ in range(owners if split else 1)] for _ in groups]
        table, picked, left, right, total = refs
        mine = lax.axis_index("rep")
        columns = lax.broadcasted_iota(jnp.int32, (width, width), 0)
        for group, order in enumerate(orders):
            names = order[...]
            for tile in range(tiles):
                place = (group * tiles + tile) * width
                hot = jnp.where(columns == names[tile : tile + 1, :], 1.0, 0.0).astype(jnp.bfloat16)
                table[:, place : place + width] = hot
        for source, sample_ref in enumerate(samples):
            used = [group for group in range(len(groups)) if groups[group][2] <= source]
            for sample in range(count):
                for part in range(2):
                    for step in range(owners):
                        owner = (((mine // 2) ^ step) * 2 + mine % 2) * rows
                        picked[part * block + step * rows : part * block + (step + 1) * rows, :] = sample_ref[
                            sample, part, pl.ds(pl.multiple_of(owner, rows), rows), :
                        ]
                real, imag = sample_ref[sample, 0], sample_ref[sample, 1]
                deep = source * step_deep + sample * 2 * width
                right[deep : deep + width, :width] = real
                right[deep : deep + width, width:] = imag
                right[deep + width : deep + 2 * width, :width] = -imag
                right[deep + width : deep + 2 * width, width:] = real
                for group in used:
                    moved = jnp.dot(
                        picked[...],
                        table[:, group * tiles * width : (group + 1) * tiles * width],
                        preferred_element_type=jnp.float32,
                    ).astype(jnp.bfloat16)
                    for tile in range(tiles):
                        for part in range(2):
                            left[
                                group * height + tile * block : group * height + (tile + 1) * block,
                                deep + part * width : deep + (part + 1) * width,
                            ] = moved[part * block : (part + 1) * block, tile * width : (tile + 1) * width]
        for group, (_, _, first) in enumerate(groups):
            start = first * step_deep
            sums = jnp.dot(
                left[group * height : (group + 1) * height, start:], right[start:, :], preferred_element_type=jnp.float32
            )
            if befores[group] is not None:
                sums = sums + befores[group][...]
            if not split:
                outs[group][0][...] = sums
                continue
            total[...] = sums
            for step in range(owners):
                for tile in range(tiles):
                    at = tile * block + step * rows
                    outs[group][step][tile * rows : (tile + 1) * rows, :] = total[at : at + rows, :]

    if split:
        out_shape = [jax.ShapeDtypeStruct((tiles * rows, 2 * width), jnp.float32)] * (len(groups) * owners)
    else:
        out_shape = [jax.ShapeDtypeStruct((height, 2 * width), jnp.float32)] * len(groups)
    operands = [group[0] for group in groups] + [group[1] for group in groups if group[1] is not None] + sources
    whole = pl.BlockSpec(memory_space=pltpu.VMEM)
    got = pl.pallas_call(
        kernel,
        out_shape=out_shape,
        in_specs=[whole] * len(operands),
        out_specs=[whole] * len(out_shape),
        scratch_shapes=[
            pltpu.VMEM((width, len(groups) * tiles * width), jnp.bfloat16),
            pltpu.VMEM((2 * block, width), jnp.bfloat16),
            pltpu.VMEM((len(groups) * height, depth), jnp.bfloat16),
            pltpu.VMEM((depth, 2 * width), jnp.bfloat16),
            pltpu.VMEM((height, 2 * width), jnp.float32),
        ],
        compiler_params=pltpu.CompilerParams(vmem_limit_bytes=VMEM_BYTES),
        cost_estimate=pl.CostEstimate(
            flops=4 * len(groups) * height * depth * 2 * width, bytes_accessed=2 * depth * width, transcendentals=0
        ),
    )(*operands)
    per = owners if split else 1
    got = [got[group * per : (group + 1) * per] for group in range(len(groups))]
    return got if split else [each[0] for each in got]


def body(rep, blk, green_samples, exchange_index_order, frequency_offset):
    tiles, width = exchange_index_order.shape
    rows = width // rep

    def over(axis, size, flip, value):
        return lax.ppermute(value, axis, [(i, i ^ flip) for i in range(size)])

    part = functools.partial(partial_tiles, rep, rows, tiles)
    near = over("blk", blk, 1, green_samples)
    twin = over("rep", rep, 1, green_samples)
    own_order = turned_order(exchange_index_order, frequency_offset)
    far_order = over("blk", blk, 2, own_order)
    (own,) = part([(own_order, None, 0)], [green_samples], False)
    near, own, far_order, twin = lax.optimization_barrier((near, own, far_order, twin))
    near_twin = over("rep", rep, 1, near)
    far, own = part([(far_order, None, 0), (own_order, own, 1)], [green_samples, twin, near], False)
    (far_parts,) = part([(far_order, far, 0)], [near_twin], True)
    (own_parts,) = part([(own_order, own, 0)], [near_twin], True)

    def collect(parts):
        value = parts[0]
        for step in range(rep // 2 - 1, 0, -1):
            value = value + over("rep", rep, 2 * step, parts[step])
        return value

    far = over("blk", blk, 2, collect(far_parts))
    done = collect(own_parts) + far
    done = done.reshape(tiles, rows, 2, width)
    return jnp.transpose(done, (2, 0, 1, 3))


def solution(mesh):
    rep, blk = mesh.shape["rep"], mesh.shape["blk"]
    placed = (P(("rep", "blk"), None, None, None), P("blk", None), P("blk"))

    def program(green_samples, exchange_index_order, frequency_offset):
        width = exchange_index_order.shape[1]
        if blk == 4 and width // rep % 16 == 0:
            part = functools.partial(body, rep, blk)
        else:
            part = plain_body
        return jax.shard_map(
            part, mesh=mesh, in_specs=placed, out_specs=P(None, "blk", "rep", None), check_vma=False
        )(green_samples, exchange_index_order, frequency_offset)

    return program
```

```python
import functools

import jax
import jax.numpy as jnp
from jax import lax
from jax.experimental import pallas as pl
from jax.experimental.pallas import tpu as pltpu
from jax.sharding import PartitionSpec as P

VMEM_BYTES = 48 * 1024 * 1024


def plain_body(green_samples, exchange_index_order, frequency_offset):
    tile_width = green_samples.shape[2]
    positions = jnp.arange(tile_width, dtype=jnp.int32)
    back_rows = (positions[None, :] - frequency_offset[:, None]) % tile_width
    composed_cols = jnp.take_along_axis(exchange_index_order, back_rows, axis=1)
    left_table = (composed_cols[:, None, :] == positions[None, :, None]).astype(jnp.bfloat16)
    tile_portion = lax.all_gather(green_samples, "blk", axis=0, tiled=True)
    left = jnp.einsum(
        "mcis,qsk->mciqk", tile_portion, left_table, preferred_element_type=jnp.float32
    ).astype(jnp.bfloat16)
    dot = functools.partial(jnp.einsum, "miqk,mkj->qij", preferred_element_type=jnp.float32)
    real_part = dot(left[:, 0], tile_portion[:, 0]) - dot(left[:, 1], tile_portion[:, 1])
    imag_part = dot(left[:, 0], tile_portion[:, 1]) + dot(left[:, 1], tile_portion[:, 0])
    stacked = jnp.stack([real_part, imag_part])
    return lax.psum_scatter(stacked, "rep", scatter_dimension=2, tiled=True)


def turned_order(order, offset):
    tiles, _ = order.shape

    def kernel(order_ref, offset_ref, out_ref):
        names = order_ref[...]
        for tile in range(tiles):
            out_ref[tile : tile + 1, :] = pltpu.roll(names, offset_ref[tile], 1)[tile : tile + 1, :]

    return pl.pallas_call(
        kernel,
        out_shape=jax.ShapeDtypeStruct(order.shape, order.dtype),
        in_specs=[pl.BlockSpec(memory_space=pltpu.VMEM), pl.BlockSpec(memory_space=pltpu.SMEM)],
        out_specs=pl.BlockSpec(memory_space=pltpu.VMEM),
    )(order, offset)


def partial_tiles(rep, rows, tiles, groups, sources, split):
    owners = rep // 2
    width = groups[0][0].shape[1]
    count = sources[0].shape[0]
    block = owners * rows
    height = tiles * block
    gathered = tiles - tiles // 4
    step_deep = count * 2 * width
    depth = len(sources) * step_deep

    def kernel(*refs):
        refs = list(refs)
        orders = [refs.pop(0) for _ in groups]
        befores = [None if group[1] is None else refs.pop(0) for group in groups]
        samples = [refs.pop(0) for _ in sources]
        outs = [[refs.pop(0) for _ in range(owners if split else 1)] for _ in groups]
        table, picked, left, right, total = refs
        mine = lax.axis_index("rep")
        columns = lax.broadcasted_iota(jnp.int32, (width, width), 0)
        for group, order in enumerate(orders):
            names = order[...]
            for tile in range(gathered, tiles):
                place = (group * tiles + tile) * width
                hot = jnp.where(columns == names[tile : tile + 1, :], 1.0, 0.0).astype(jnp.bfloat16)
                table[:, place : place + width] = hot
        for source, sample_ref in enumerate(samples):
            used = [group for group in range(len(groups)) if groups[group][2] <= source]
            for sample in range(count):
                high = (source * count + sample) * 2 * block
                for part in range(2):
                    for step in range(owners):
                        owner = (((mine // 2) ^ step) * 2 + mine % 2) * rows
                        picked[high + part * block + step * rows : high + part * block + (step + 1) * rows, :] = sample_ref[
                            sample, part, pl.ds(pl.multiple_of(owner, rows), rows), :
                        ]
                real, imag = sample_ref[sample, 0], sample_ref[sample, 1]
                deep = source * step_deep + sample * 2 * width
                right[deep : deep + width, :width] = real
                right[deep : deep + width, width:] = imag
                right[deep + width : deep + 2 * width, :width] = -imag
                right[deep + width : deep + 2 * width, width:] = real
                wide = [
                    picked[high + part * block : high + (part + 1) * block, :].astype(jnp.float32) for part in range(2)
                ]
                for group in used:
                    lots = group * tiles
                    moved = None
                    if gathered < tiles:
                        moved = jnp.dot(
                            picked[high : high + 2 * block, :],
                            table[:, (lots + gathered) * width : (lots + tiles) * width],
                            preferred_element_type=jnp.float32,
                        ).astype(jnp.bfloat16)
                    for tile in range(tiles):
                        names = jnp.broadcast_to(orders[group][tile : tile + 1, :], (block, width))
                        for part in range(2):
                            if tile < gathered:
                                value = jnp.take_along_axis(wide[part], names, axis=1).astype(jnp.bfloat16)
                            else:
                                value = moved[
                                    part * block : (part + 1) * block,
                                    (tile - gathered) * width : (tile - gathered + 1) * width,
                                ]
                            left[
                                group * height + tile * block : group * height + (tile + 1) * block,
                                deep + part * width : deep + (part + 1) * width,
                            ] = value
        for group, (_, _, first) in enumerate(groups):
            start = first * step_deep
            sums = jnp.dot(
                left[group * height : (group + 1) * height, start:], right[start:, :], preferred_element_type=jnp.float32
            )
            if befores[group] is not None:
                sums = sums + befores[group][...]
            if not split:
                outs[group][0][...] = sums
                continue
            total[...] = sums
            for step in range(owners):
                for tile in range(tiles):
                    at = tile * block + step * rows
                    outs[group][step][tile * rows : (tile + 1) * rows, :] = total[at : at + rows, :]

    if split:
        out_shape = [jax.ShapeDtypeStruct((tiles * rows, 2 * width), jnp.float32)] * (len(groups) * owners)
    else:
        out_shape = [jax.ShapeDtypeStruct((height, 2 * width), jnp.float32)] * len(groups)
    operands = [group[0] for group in groups] + [group[1] for group in groups if group[1] is not None] + sources
    whole = pl.BlockSpec(memory_space=pltpu.VMEM)
    got = pl.pallas_call(
        kernel,
        out_shape=out_shape,
        in_specs=[whole] * len(operands),
        out_specs=[whole] * len(out_shape),
        scratch_shapes=[
            pltpu.VMEM((width, len(groups) * tiles * width), jnp.bfloat16),
            pltpu.VMEM((len(sources) * count * 2 * block, width), jnp.bfloat16),
            pltpu.VMEM((len(groups) * height, depth), jnp.bfloat16),
            pltpu.VMEM((depth, 2 * width), jnp.bfloat16),
            pltpu.VMEM((height, 2 * width), jnp.float32),
        ],
        compiler_params=pltpu.CompilerParams(vmem_limit_bytes=VMEM_BYTES),
        cost_estimate=pl.CostEstimate(
            flops=4 * len(groups) * height * depth * 2 * width, bytes_accessed=2 * depth * width, transcendentals=0
        ),
    )(*operands)
    per = owners if split else 1
    got = [got[group * per : (group + 1) * per] for group in range(len(groups))]
    return got if split else [each[0] for each in got]


def body(rep, blk, green_samples, exchange_index_order, frequency_offset):
    tiles, width = exchange_index_order.shape
    rows = width // rep

    def over(axis, size, flip, value):
        return lax.ppermute(value, axis, [(i, i ^ flip) for i in range(size)])

    part = functools.partial(partial_tiles, rep, rows, tiles)
    near = over("blk", blk, 1, green_samples)
    twin = over("rep", rep, 1, green_samples)
    own_order = turned_order(exchange_index_order, frequency_offset)
    far_order = over("blk", blk, 2, own_order)
    (own,) = part([(own_order, None, 0)], [green_samples], False)
    near, own, far_order, twin = lax.optimization_barrier((near, own, far_order, twin))
    near_twin = over("rep", rep, 1, near)
    far, own = part([(far_order, None, 0), (own_order, own, 1)], [green_samples, twin, near], False)
    (far_parts,) = part([(far_order, far, 0)], [near_twin], True)
    (own_parts,) = part([(own_order, own, 0)], [near_twin], True)

    def collect(parts):
        value = parts[0]
        for step in range(rep // 2 - 1, 0, -1):
            value = value + over("rep", rep, 2 * step, parts[step])
        return value

    far = over("blk", blk, 2, collect(far_parts))
    done = collect(own_parts) + far
    done = done.reshape(tiles, rows, 2, width)
    return jnp.transpose(done, (2, 0, 1, 3))


def solution(mesh):
    rep, blk = mesh.shape["rep"], mesh.shape["blk"]
    placed = (P(("rep", "blk"), None, None, None), P("blk", None), P("blk"))

    def program(green_samples, exchange_index_order, frequency_offset):
        width = exchange_index_order.shape[1]
        if blk == 4 and width // rep % 16 == 0:
            part = functools.partial(body, rep, blk)
        else:
            part = plain_body
        return jax.shard_map(
            part, mesh=mesh, in_specs=placed, out_specs=P(None, "blk", "rep", None), check_vma=False
        )(green_samples, exchange_index_order, frequency_offset)

    return program
```

```python
import functools

import jax
import jax.numpy as jnp
from jax import lax
from jax.experimental import pallas as pl
from jax.experimental.pallas import tpu as pltpu
from jax.sharding import PartitionSpec as P

VMEM_BYTES = 48 * 1024 * 1024


def plain_body(green_samples, exchange_index_order, frequency_offset):
    tile_width = green_samples.shape[2]
    positions = jnp.arange(tile_width, dtype=jnp.int32)
    back_rows = (positions[None, :] - frequency_offset[:, None]) % tile_width
    composed_cols = jnp.take_along_axis(exchange_index_order, back_rows, axis=1)
    left_table = (composed_cols[:, None, :] == positions[None, :, None]).astype(jnp.bfloat16)
    tile_portion = lax.all_gather(green_samples, "blk", axis=0, tiled=True)
    left = jnp.einsum(
        "mcis,qsk->mciqk", tile_portion, left_table, preferred_element_type=jnp.float32
    ).astype(jnp.bfloat16)
    dot = functools.partial(jnp.einsum, "miqk,mkj->qij", preferred_element_type=jnp.float32)
    real_part = dot(left[:, 0], tile_portion[:, 0]) - dot(left[:, 1], tile_portion[:, 1])
    imag_part = dot(left[:, 0], tile_portion[:, 1]) + dot(left[:, 1], tile_portion[:, 0])
    stacked = jnp.stack([real_part, imag_part])
    return lax.psum_scatter(stacked, "rep", scatter_dimension=2, tiled=True)


def turned_order(order, offset):
    tiles, _ = order.shape

    def kernel(order_ref, offset_ref, out_ref):
        names = order_ref[...]
        for tile in range(tiles):
            out_ref[tile : tile + 1, :] = pltpu.roll(names, offset_ref[tile], 1)[tile : tile + 1, :]

    return pl.pallas_call(
        kernel,
        out_shape=pltpu.VMEM(order.shape, order.dtype),
        in_specs=[pl.BlockSpec(memory_space=pltpu.VMEM), pl.BlockSpec(memory_space=pltpu.SMEM)],
        out_specs=pl.BlockSpec(memory_space=pltpu.VMEM),
    )(order, offset)


def partial_tiles(rep, rows, tiles, groups, sources, split):
    owners = rep // 2
    width = groups[0][0].shape[1]
    count = sources[0].shape[0]
    block = owners * rows
    height = tiles * block
    gathered = tiles - tiles // 4
    step_deep = count * 2 * width
    depth = len(sources) * step_deep

    def kernel(*refs):
        refs = list(refs)
        orders = [refs.pop(0) for _ in groups]
        befores = [None if group[1] is None else refs.pop(0) for group in groups]
        samples = [refs.pop(0) for _ in sources]
        outs = [[refs.pop(0) for _ in range(owners if split else 1)] for _ in groups]
        table, picked, left, right = refs
        mine = lax.axis_index("rep")
        columns = lax.broadcasted_iota(jnp.int32, (width, width), 0)
        for group, order in enumerate(orders):
            names = order[...]
            for tile in range(gathered, tiles):
                place = (group * tiles + tile) * width
                hot = jnp.where(columns == names[tile : tile + 1, :], 1.0, 0.0).astype(jnp.bfloat16)
                table[:, place : place + width] = hot
        for source, sample_ref in enumerate(samples):
            used = [group for group in range(len(groups)) if groups[group][2] <= source]
            for sample in range(count):
                high = (source * count + sample) * 2 * block
                for part in range(2):
                    for step in range(owners):
                        owner = (((mine // 2) ^ step) * 2 + mine % 2) * rows
                        picked[high + part * block + step * rows : high + part * block + (step + 1) * rows, :] = sample_ref[
                            sample, part, pl.ds(pl.multiple_of(owner, rows), rows), :
                        ]
                real, imag = sample_ref[sample, 0], sample_ref[sample, 1]
                deep = source * step_deep + sample * 2 * width
                right[deep : deep + width, :width] = real
                right[deep : deep + width, width:] = imag
                right[deep + width : deep + 2 * width, :width] = -imag
                right[deep + width : deep + 2 * width, width:] = real
                wide = [
                    picked[high + part * block : high + (part + 1) * block, :].astype(jnp.float32) for part in range(2)
                ]
                for group in used:
                    lots = group * tiles
                    moved = None
                    if gathered < tiles:
                        moved = jnp.dot(
                            picked[high : high + 2 * block, :],
                            table[:, (lots + gathered) * width : (lots + tiles) * width],
                            preferred_element_type=jnp.float32,
                        ).astype(jnp.bfloat16)
                    for tile in range(tiles):
                        names = jnp.broadcast_to(orders[group][tile : tile + 1, :], (block, width))
                        for part in range(2):
                            if tile < gathered:
                                value = jnp.take_along_axis(wide[part], names, axis=1).astype(jnp.bfloat16)
                            else:
                                value = moved[
                                    part * block : (part + 1) * block,
                                    (tile - gathered) * width : (tile - gathered + 1) * width,
                                ]
                            left[
                                group * height + tile * block : group * height + (tile + 1) * block,
                                deep + part * width : deep + (part + 1) * width,
                            ] = value
        for group, (_, _, first) in enumerate(groups):
            start = first * step_deep
            sums = jnp.dot(
                left[group * height : (group + 1) * height, start:], right[start:, :], preferred_element_type=jnp.float32
            )
            if befores[group] is not None:
                sums = sums + befores[group][...]
            if not split:
                outs[group][0][...] = sums
                continue
            for step in range(owners):
                for tile in range(tiles):
                    at = tile * block + step * rows
                    outs[group][step][tile * rows : (tile + 1) * rows, :] = sums[at : at + rows, :]

    if split:
        out_shape = [jax.ShapeDtypeStruct((tiles * rows, 2 * width), jnp.float32)] * (len(groups) * owners)
    else:
        out_shape = [jax.ShapeDtypeStruct((height, 2 * width), jnp.float32)] * len(groups)
    operands = [group[0] for group in groups] + [group[1] for group in groups if group[1] is not None] + sources
    whole = pl.BlockSpec(memory_space=pltpu.VMEM)
    got = pl.pallas_call(
        kernel,
        out_shape=out_shape,
        in_specs=[whole] * len(operands),
        out_specs=[whole] * len(out_shape),
        scratch_shapes=[
            pltpu.VMEM((width, len(groups) * tiles * width), jnp.bfloat16),
            pltpu.VMEM((len(sources) * count * 2 * block, width), jnp.bfloat16),
            pltpu.VMEM((len(groups) * height, depth), jnp.bfloat16),
            pltpu.VMEM((depth, 2 * width), jnp.bfloat16),
        ],
        compiler_params=pltpu.CompilerParams(vmem_limit_bytes=VMEM_BYTES),
        cost_estimate=pl.CostEstimate(
            flops=4 * len(groups) * height * depth * 2 * width, bytes_accessed=2 * depth * width, transcendentals=0
        ),
    )(*operands)
    per = owners if split else 1
    got = [got[group * per : (group + 1) * per] for group in range(len(groups))]
    return got if split else [each[0] for each in got]


def body(rep, blk, green_samples, exchange_index_order, frequency_offset):
    tiles, width = exchange_index_order.shape
    rows = width // rep

    def over(axis, size, flip, value):
        return lax.ppermute(value, axis, [(i, i ^ flip) for i in range(size)])

    part = functools.partial(partial_tiles, rep, rows, tiles)
    flips = range(2, blk, 2)
    near = over("blk", blk, 1, green_samples)
    twin = over("rep", rep, 1, green_samples)
    own_order = turned_order(exchange_index_order, frequency_offset)
    far_orders = [over("blk", blk, flip, own_order) for flip in flips]
    (own,) = part([(own_order, None, 0)], [green_samples], False)
    near, own, far_orders, twin = lax.optimization_barrier((near, own, far_orders, twin))
    near_twin = over("rep", rep, 1, near)
    *fars, own = part(
        [(order, None, 0) for order in far_orders] + [(own_order, own, 1)], [green_samples, twin, near], False
    )

    def collect(order, sums):
        (parts,) = part([(order, sums, 0)], [near_twin], True)
        value = parts[0]
        for step in range(rep // 2 - 1, 0, -1):
            value = value + over("rep", rep, 2 * step, parts[step])
        return value

    others = [over("blk", blk, flip, collect(*each)) for flip, *each in zip(flips, far_orders, fars)]
    done = collect(own_order, own)
    for other in others:
        done = done + other
    done = done.reshape(tiles, rows, 2, width)
    return jnp.transpose(done, (2, 0, 1, 3))


def solution(mesh):
    rep, blk = mesh.shape["rep"], mesh.shape["blk"]
    placed = (P(("rep", "blk"), None, None, None), P("blk", None), P("blk"))

    def program(green_samples, exchange_index_order, frequency_offset):
        width = exchange_index_order.shape[1]
        if rep & (rep - 1) == 0 and blk & (blk - 1) == 0 and min(rep, blk) > 1 and width // rep % 16 == 0:
            part = functools.partial(body, rep, blk)
        else:
            part = plain_body
        return jax.shard_map(
            part, mesh=mesh, in_specs=placed, out_specs=P(None, "blk", "rep", None), check_vma=False
        )(green_samples, exchange_index_order, frequency_offset)

    return program
```

```python
import functools

import jax
import jax.numpy as jnp
from jax import lax
from jax.experimental import pallas as pl
from jax.experimental.pallas import tpu as pltpu
from jax.sharding import PartitionSpec as P

VMEM_BYTES = 48 * 1024 * 1024


def plain_body(green_samples, exchange_index_order, frequency_offset):
    tile_width = green_samples.shape[2]
    positions = jnp.arange(tile_width, dtype=jnp.int32)
    back_rows = (positions[None, :] - frequency_offset[:, None]) % tile_width
    composed_cols = jnp.take_along_axis(exchange_index_order, back_rows, axis=1)
    left_table = (composed_cols[:, None, :] == positions[None, :, None]).astype(jnp.bfloat16)
    tile_portion = lax.all_gather(green_samples, "blk", axis=0, tiled=True)
    left = jnp.einsum(
        "mcis,qsk->mciqk", tile_portion, left_table, preferred_element_type=jnp.float32
    ).astype(jnp.bfloat16)
    dot = functools.partial(jnp.einsum, "miqk,mkj->qij", preferred_element_type=jnp.float32)
    real_part = dot(left[:, 0], tile_portion[:, 0]) - dot(left[:, 1], tile_portion[:, 1])
    imag_part = dot(left[:, 0], tile_portion[:, 1]) + dot(left[:, 1], tile_portion[:, 0])
    stacked = jnp.stack([real_part, imag_part])
    return lax.psum_scatter(stacked, "rep", scatter_dimension=2, tiled=True)


def turned_order(order, offset):
    tiles, _ = order.shape

    def kernel(order_ref, offset_ref, out_ref):
        names = order_ref[...]
        for tile in range(tiles):
            out_ref[tile : tile + 1, :] = pltpu.roll(names, offset_ref[tile], 1)[tile : tile + 1, :]

    return pl.pallas_call(
        kernel,
        out_shape=pltpu.VMEM(order.shape, order.dtype),
        in_specs=[pl.BlockSpec(memory_space=pltpu.VMEM), pl.BlockSpec(memory_space=pltpu.SMEM)],
        out_specs=pl.BlockSpec(memory_space=pltpu.VMEM),
    )(order, offset)


def owner_of(rep, mine, step):
    chip, core = mine // 2, mine % 2
    turned = step % (rep // 2 - 1) + 1 if step else 0
    return (chip ^ (step + core * (turned - step))) * 2 + core


def partial_tiles(rep, rows, tiles, groups, sources, split):
    owners = rep // 2
    width = groups[0][0].shape[1]
    count = sources[0].shape[0]
    block = owners * rows
    height = tiles * block
    gathered = tiles - tiles // 4
    step_deep = count * 2 * width
    depth = len(sources) * step_deep

    def kernel(*refs):
        refs = list(refs)
        orders = [refs.pop(0) for _ in groups]
        befores = [None if group[1] is None else refs.pop(0) for group in groups]
        samples = [refs.pop(0) for _ in sources]
        outs = [[refs.pop(0) for _ in range(owners if split else 1)] for _ in groups]
        table, picked, left, right = refs
        mine = lax.axis_index("rep")
        columns = lax.broadcasted_iota(jnp.int32, (width, width), 0)
        for group, order in enumerate(orders):
            names = order[...]
            for tile in range(gathered, tiles):
                place = (group * tiles + tile) * width
                hot = jnp.where(columns == names[tile : tile + 1, :], 1.0, 0.0).astype(jnp.bfloat16)
                table[:, place : place + width] = hot
        for source, sample_ref in enumerate(samples):
            used = [group for group in range(len(groups)) if groups[group][2] <= source]
            for sample in range(count):
                high = (source * count + sample) * 2 * block
                for part in range(2):
                    for step in range(owners):
                        owner = owner_of(rep, mine, step) * rows
                        picked[high + part * block + step * rows : high + part * block + (step + 1) * rows, :] = sample_ref[
                            sample, part, pl.ds(pl.multiple_of(owner, rows), rows), :
                        ]
                real, imag = sample_ref[sample, 0], sample_ref[sample, 1]
                deep = source * step_deep + sample * 2 * width
                right[deep : deep + width, :width] = real
                right[deep : deep + width, width:] = imag
                right[deep + width : deep + 2 * width, :width] = -imag
                right[deep + width : deep + 2 * width, width:] = real
                wide = [
                    picked[high + part * block : high + (part + 1) * block, :].astype(jnp.float32) for part in range(2)
                ]
                for group in used:
                    lots = group * tiles
                    moved = None
                    if gathered < tiles:
                        moved = jnp.dot(
                            picked[high : high + 2 * block, :],
                            table[:, (lots + gathered) * width : (lots + tiles) * width],
                            preferred_element_type=jnp.float32,
                        ).astype(jnp.bfloat16)
                    for tile in range(tiles):
                        names = jnp.broadcast_to(orders[group][tile : tile + 1, :], (block, width))
                        for part in range(2):
                            if tile < gathered:
                                value = jnp.take_along_axis(wide[part], names, axis=1).astype(jnp.bfloat16)
                            else:
                                value = moved[
                                    part * block : (part + 1) * block,
                                    (tile - gathered) * width : (tile - gathered + 1) * width,
                                ]
                            left[
                                group * height + tile * block : group * height + (tile + 1) * block,
                                deep + part * width : deep + (part + 1) * width,
                            ] = value
        for group, (_, _, first) in enumerate(groups):
            start = first * step_deep
            sums = jnp.dot(
                left[group * height : (group + 1) * height, start:], right[start:, :], preferred_element_type=jnp.float32
            )
            if befores[group] is not None:
                sums = sums + befores[group][...]
            if not split:
                outs[group][0][...] = sums
                continue
            for step in range(owners):
                for tile in range(tiles):
                    at = tile * block + step * rows
                    outs[group][step][tile * rows : (tile + 1) * rows, :] = sums[at : at + rows, :]

    if split:
        out_shape = [jax.ShapeDtypeStruct((tiles * rows, 2 * width), jnp.float32)] * (len(groups) * owners)
    else:
        out_shape = [jax.ShapeDtypeStruct((height, 2 * width), jnp.float32)] * len(groups)
    operands = [group[0] for group in groups] + [group[1] for group in groups if group[1] is not None] + sources
    whole = pl.BlockSpec(memory_space=pltpu.VMEM)
    got = pl.pallas_call(
        kernel,
        out_shape=out_shape,
        in_specs=[whole] * len(operands),
        out_specs=[whole] * len(out_shape),
        scratch_shapes=[
            pltpu.VMEM((width, len(groups) * tiles * width), jnp.bfloat16),
            pltpu.VMEM((len(sources) * count * 2 * block, width), jnp.bfloat16),
            pltpu.VMEM((len(groups) * height, depth), jnp.bfloat16),
            pltpu.VMEM((depth, 2 * width), jnp.bfloat16),
        ],
        compiler_params=pltpu.CompilerParams(vmem_limit_bytes=VMEM_BYTES),
        cost_estimate=pl.CostEstimate(
            flops=4 * len(groups) * height * depth * 2 * width, bytes_accessed=2 * depth * width, transcendentals=0
        ),
    )(*operands)
    per = owners if split else 1
    got = [got[group * per : (group + 1) * per] for group in range(len(groups))]
    return got if split else [each[0] for each in got]


def body(rep, blk, green_samples, exchange_index_order, frequency_offset):
    tiles, width = exchange_index_order.shape
    rows = width // rep

    def over(axis, size, flip, value):
        return lax.ppermute(value, axis, [(i, i ^ flip) for i in range(size)])

    part = functools.partial(partial_tiles, rep, rows, tiles)
    flips = range(2, blk, 2)
    near = over("blk", blk, 1, green_samples)
    twin = over("rep", rep, 1, green_samples)
    own_order = turned_order(exchange_index_order, frequency_offset)
    far_orders = [over("blk", blk, flip, own_order) for flip in flips]
    (own,) = part([(own_order, None, 0)], [green_samples], False)
    near, own, far_orders, twin = lax.optimization_barrier((near, own, far_orders, twin))
    near_twin = over("rep", rep, 1, near)
    *fars, own = part(
        [(order, None, 0) for order in far_orders] + [(own_order, own, 1)], [green_samples, twin, near], False
    )

    def collect(order, sums):
        (parts,) = part([(order, sums, 0)], [near_twin], True)
        value = parts[0]
        for step in range(rep // 2 - 1, 0, -1):
            value = value + lax.ppermute(parts[step], "rep", [(i, owner_of(rep, i, step)) for i in range(rep)])
        return value

    others = [over("blk", blk, flip, collect(*each)) for flip, *each in zip(flips, far_orders, fars)]
    done = collect(own_order, own)
    for other in others:
        done = done + other
    done = done.reshape(tiles, rows, 2, width)
    return jnp.transpose(done, (2, 0, 1, 3))


def solution(mesh):
    rep, blk = mesh.shape["rep"], mesh.shape["blk"]
    placed = (P(("rep", "blk"), None, None, None), P("blk", None), P("blk"))

    def program(green_samples, exchange_index_order, frequency_offset):
        width = exchange_index_order.shape[1]
        if rep & (rep - 1) == 0 and blk & (blk - 1) == 0 and min(rep, blk) > 1 and width // rep % 16 == 0:
            part = functools.partial(body, rep, blk)
        else:
            part = plain_body
        return jax.shard_map(
            part, mesh=mesh, in_specs=placed, out_specs=P(None, "blk", "rep", None), check_vma=False
        )(green_samples, exchange_index_order, frequency_offset)

    return program
```

```python
import functools

import jax
import jax.numpy as jnp
from jax import lax
from jax.experimental import pallas as pl
from jax.experimental.pallas import tpu as pltpu
from jax.sharding import PartitionSpec as P

VMEM_BYTES = 48 * 1024 * 1024


def plain_body(green_samples, exchange_index_order, frequency_offset):
    tile_width = green_samples.shape[2]
    positions = jnp.arange(tile_width, dtype=jnp.int32)
    back_rows = (positions[None, :] - frequency_offset[:, None]) % tile_width
    composed_cols = jnp.take_along_axis(exchange_index_order, back_rows, axis=1)
    left_table = (composed_cols[:, None, :] == positions[None, :, None]).astype(jnp.bfloat16)
    tile_portion = lax.all_gather(green_samples, "blk", axis=0, tiled=True)
    left = jnp.einsum(
        "mcis,qsk->mciqk", tile_portion, left_table, preferred_element_type=jnp.float32
    ).astype(jnp.bfloat16)
    dot = functools.partial(jnp.einsum, "miqk,mkj->qij", preferred_element_type=jnp.float32)
    real_part = dot(left[:, 0], tile_portion[:, 0]) - dot(left[:, 1], tile_portion[:, 1])
    imag_part = dot(left[:, 0], tile_portion[:, 1]) + dot(left[:, 1], tile_portion[:, 0])
    stacked = jnp.stack([real_part, imag_part])
    return lax.psum_scatter(stacked, "rep", scatter_dimension=2, tiled=True)


def turned_order(order, offset):
    tiles, _ = order.shape

    def kernel(order_ref, offset_ref, out_ref):
        names = order_ref[...]
        for tile in range(tiles):
            out_ref[tile : tile + 1, :] = pltpu.roll(names, offset_ref[tile], 1)[tile : tile + 1, :]

    return pl.pallas_call(
        kernel,
        out_shape=pltpu.VMEM(order.shape, order.dtype),
        in_specs=[pl.BlockSpec(memory_space=pltpu.VMEM), pl.BlockSpec(memory_space=pltpu.SMEM)],
        out_specs=pl.BlockSpec(memory_space=pltpu.VMEM),
    )(order, offset)


def owner_of(rep, mine, step):
    chip, core = mine // 2, mine % 2
    turned = step % (rep // 2 - 1) + 1 if step else 0
    return (chip ^ (step + core * (turned - step))) * 2 + core


def partial_tiles(rep, rows, tiles, groups, sources, split):
    owners = rep // 2
    width = groups[0][0].shape[1]
    count = sources[0].shape[0]
    block = owners * rows
    height = tiles * block
    gathered = tiles - tiles // 4
    step_deep = count * 2 * width
    depth = len(sources) * step_deep

    def kernel(*refs):
        refs = list(refs)
        orders = [refs.pop(0) for _ in groups]
        befores = [None if group[1] is None else refs.pop(0) for group in groups]
        samples = [refs.pop(0) for _ in sources]
        outs = [[refs.pop(0) for _ in range(owners if split else 1)] for _ in groups]
        table, picked, left, right = refs
        mine = lax.axis_index("rep")
        columns = lax.broadcasted_iota(jnp.int32, (width, width), 0)
        for group, order in enumerate(orders):
            names = order[...]
            for tile in range(gathered, tiles):
                place = (group * tiles + tile) * width
                hot = jnp.where(columns == names[tile : tile + 1, :], 1.0, 0.0).astype(jnp.bfloat16)
                table[:, place : place + width] = hot
        for source, sample_ref in enumerate(samples):
            used = [group for group in range(len(groups)) if groups[group][2] <= source]
            for sample in range(count):
                high = (source * count + sample) * 2 * block
                for part in range(2):
                    for step in range(owners):
                        owner = owner_of(rep, mine, step) * rows
                        picked[high + part * block + step * rows : high + part * block + (step + 1) * rows, :] = sample_ref[
                            sample, part, pl.ds(pl.multiple_of(owner, rows), rows), :
                        ]
                real, imag = sample_ref[sample, 0], sample_ref[sample, 1]
                deep = source * step_deep + sample * 2 * width
                right[deep : deep + width, :width] = real
                right[deep : deep + width, width:] = imag
                right[deep + width : deep + 2 * width, :width] = -imag
                right[deep + width : deep + 2 * width, width:] = real
                wide = [
                    picked[high + part * block : high + (part + 1) * block, :].astype(jnp.float32) for part in range(2)
                ]
                for group in used:
                    lots = group * tiles
                    moved = None
                    if gathered < tiles:
                        moved = jnp.dot(
                            picked[high : high + 2 * block, :],
                            table[:, (lots + gathered) * width : (lots + tiles) * width],
                            preferred_element_type=jnp.float32,
                        ).astype(jnp.bfloat16)
                    for tile in range(tiles):
                        names = jnp.broadcast_to(orders[group][tile : tile + 1, :], (block, width))
                        for part in range(2):
                            if tile < gathered:
                                value = jnp.take_along_axis(wide[part], names, axis=1).astype(jnp.bfloat16)
                            else:
                                value = moved[
                                    part * block : (part + 1) * block,
                                    (tile - gathered) * width : (tile - gathered + 1) * width,
                                ]
                            left[
                                group * height + tile * block : group * height + (tile + 1) * block,
                                deep + part * width : deep + (part + 1) * width,
                            ] = value
        for group, (_, _, first) in enumerate(groups):
            start = first * step_deep
            sums = jnp.dot(
                left[group * height : (group + 1) * height, start:], right[start:, :], preferred_element_type=jnp.float32
            )
            if befores[group] is not None:
                sums = sums + befores[group][...]
            if not split:
                outs[group][0][...] = sums
                continue
            for step in range(owners):
                for tile in range(tiles):
                    at = tile * block + step * rows
                    for part in range(2):
                        to = (part * tiles + tile) * rows
                        outs[group][step][to : to + rows, :] = sums[at : at + rows, part * width : (part + 1) * width]

    if split:
        out_shape = [jax.ShapeDtypeStruct((2 * tiles * rows, width), jnp.float32)] * (len(groups) * owners)
    else:
        out_shape = [jax.ShapeDtypeStruct((height, 2 * width), jnp.float32)] * len(groups)
    operands = [group[0] for group in groups] + [group[1] for group in groups if group[1] is not None] + sources
    whole = pl.BlockSpec(memory_space=pltpu.VMEM)
    got = pl.pallas_call(
        kernel,
        out_shape=out_shape,
        in_specs=[whole] * len(operands),
        out_specs=[whole] * len(out_shape),
        scratch_shapes=[
            pltpu.VMEM((width, len(groups) * tiles * width), jnp.bfloat16),
            pltpu.VMEM((len(sources) * count * 2 * block, width), jnp.bfloat16),
            pltpu.VMEM((len(groups) * height, depth), jnp.bfloat16),
            pltpu.VMEM((depth, 2 * width), jnp.bfloat16),
        ],
        compiler_params=pltpu.CompilerParams(vmem_limit_bytes=VMEM_BYTES),
        cost_estimate=pl.CostEstimate(
            flops=4 * len(groups) * height * depth * 2 * width, bytes_accessed=2 * depth * width, transcendentals=0
        ),
    )(*operands)
    per = owners if split else 1
    got = [got[group * per : (group + 1) * per] for group in range(len(groups))]
    return got if split else [each[0] for each in got]


def body(rep, blk, green_samples, exchange_index_order, frequency_offset):
    tiles, width = exchange_index_order.shape
    rows = width // rep

    def over(axis, size, flip, value):
        return lax.ppermute(value, axis, [(i, i ^ flip) for i in range(size)])

    part = functools.partial(partial_tiles, rep, rows, tiles)
    flips = range(2, blk, 2)
    near = over("blk", blk, 1, green_samples)
    twin = over("rep", rep, 1, green_samples)
    own_order = turned_order(exchange_index_order, frequency_offset)
    far_orders = [over("blk", blk, flip, own_order) for flip in flips]
    (own,) = part([(own_order, None, 0)], [green_samples], False)
    near, own, far_orders, twin = lax.optimization_barrier((near, own, far_orders, twin))
    near_twin = over("rep", rep, 1, near)
    *fars, own = part(
        [(order, None, 0) for order in far_orders] + [(own_order, own, 1)], [green_samples, twin, near], False
    )

    def collect(order, sums):
        (parts,) = part([(order, sums, 0)], [near_twin], True)
        value = parts[0]
        for step in range(rep // 2 - 1, 0, -1):
            value = value + lax.ppermute(parts[step], "rep", [(i, owner_of(rep, i, step)) for i in range(rep)])
        return value

    others = [over("blk", blk, flip, collect(*each)) for flip, *each in zip(flips, far_orders, fars)]
    done = collect(own_order, own)
    for other in others:
        done = done + other
    return done.reshape(2, tiles, rows, width)


def solution(mesh):
    rep, blk = mesh.shape["rep"], mesh.shape["blk"]
    placed = (P(("rep", "blk"), None, None, None), P("blk", None), P("blk"))

    def program(green_samples, exchange_index_order, frequency_offset):
        width = exchange_index_order.shape[1]
        if rep & (rep - 1) == 0 and blk & (blk - 1) == 0 and min(rep, blk) > 1 and width // rep % 16 == 0:
            part = functools.partial(body, rep, blk)
        else:
            part = plain_body
        return jax.shard_map(
            part, mesh=mesh, in_specs=placed, out_specs=P(None, "blk", "rep", None), check_vma=False
        )(green_samples, exchange_index_order, frequency_offset)

    return program
```
